512 devices in a mesh: tm: 8 (over z_hi, core), tile: 16 (over x, y), head: 4 (over z_lo).
Axes of the slice: x: 4, y: 4, z: 16 (z_hi: 4, z_lo: 4; z = z_hi * 4 + z_lo), core: 2. Of those that a mesh axis runs over, the one named last changes fastest.
Arguments:
- query: bfloat16 [8, 16, 2, 16, 16, 1536], P('tm', 'tile', None, None, None, 'head'), may hold values from -80 to 80
- keys: bfloat16 [8, 16, 2, 16, 16, 1536], P('tm', 'tile', None, None, None, 'head'), may hold values from -80 to 80
- values: bfloat16 [8, 16, 2, 16, 16, 1536], P('tm', 'tile', None, None, None, 'head'), may hold values from -6 to 6
- out_weight: bfloat16 [1536, 1536], P('head'), may hold values from -0.15625 to 0.15625
- radius: int32 [12], P('head'), may hold values from 1 to 4
- block_mask: int32 [12, 8, 8], P('head'), may hold values from 0 to 1, as said below
Outputs:
- mixed: bfloat16 [8, 16, 512, 1536], P('tm', 'tile', 'head')
The draws below stay inside these ranges and needn't reach their ends.
Inputs may be any that keep to these rules, and one draw needn't show every extreme that they name: For every head, block_mask is 1 on the diagonal of its table and 0 above it.
All inputs are finite; a program needn't handle non-finite values.
Results may differ from the reference program's by a relative error of at most 0.015.
Values may be sent and summed in bfloat16 or wider, within the bound.
A program may use at most 128 MiB of HBM per device.

```python
import math
import jax
import jax.numpy as jnp
import numpy as np
from jax import lax

D = 1536
HEADS = 12
HD = 128
FRAMES = 2
TH = 16
TW = 16
RMAX = 4
NC = 8
TILES = 16
TOK = 512
N_TM = 8
N_TILE = 16


def paired_fields(key):
    shape = (N_TM, N_TILE, FRAMES, TH, TW, HEADS * HD)
    query = jax.random.normal(jax.random.fold_in(key, 101), shape, jnp.float32)
    keys = jax.random.normal(jax.random.fold_in(key, 202), shape, jnp.float32)
    return (jnp.clip(query, -80.0, 80.0), jnp.clip(keys, -80.0, 80.0))


def draw_query(key, part):
    return paired_fields(key)[0].astype(jnp.bfloat16)


def draw_keys(key, part):
    return paired_fields(key)[1].astype(jnp.bfloat16)


def draw_block_mask(key, part):
    shape = (HEADS, N_TM, N_TM)
    coins = jax.random.randint(jax.random.fold_in(key, 404), shape, 0, 2)
    rows_at = lax.broadcasted_iota(jnp.int32, shape, 1)
    cols_at = lax.broadcasted_iota(jnp.int32, shape, 2)
    below = jnp.where(rows_at > cols_at, coins, 0)
    return jnp.where(rows_at == cols_at, 1, below).astype(jnp.int32)


def touch_ends(drawn, rng, low, largest):
    longest = drawn.shape.index(max(drawn.shape))
    spots = []
    for shift in (0, 1):
        where = [jax.random.randint(jax.random.fold_in(rng, axis), (), 0, length) for axis, length in enumerate(drawn.shape)]
        where[longest] = (where[longest] + shift) % drawn.shape[longest]
        spots.append(tuple(where))
    return drawn.at[spots[0]].set(low).at[spots[1]].set(largest)


def shard_levels(key, shape, pieces, least, largest):
    def one(dim, blocks):
        draws = jax.random.uniform(jax.random.fold_in(jax.random.fold_in(key, 6), dim), (blocks,), jnp.float32, least / len(pieces), largest / len(pieces))
        return jnp.repeat(jnp.exp(draws), shape[dim] // blocks).reshape((-1,) + (1,) * (len(shape) - dim - 1))

    loudness = one(*pieces[0])
    for cut in pieces[1:]:
        loudness = loudness * one(*cut)
    return loudness


def normal_values(rng, extent, scale, bound, shards=(), kind=jnp.bfloat16):
    loudness = shard_levels(rng, extent, shards, -0.22, 0.18) if shards else 1.0
    entries = jax.random.normal(rng, extent, jnp.float32) * scale * loudness
    return jnp.minimum(jnp.maximum(entries, -bound), bound).astype(kind)


def setup_inputs(seed: int = 0) -> dict:
    streams_of = jax.random.split(jax.random.key(seed), 7)
    query = draw_query(jax.random.fold_in(streams_of[6], 71), 0)
    keys = draw_keys(jax.random.fold_in(streams_of[6], 71), 0)
    values = normal_values(streams_of[2], (NC, TILES, FRAMES, TH, TW, HEADS * HD), 1.0, 6.0, ((0, 8), (1, 16), (5, 4)))
    out_weight = normal_values(streams_of[3], (HEADS * HD, D), (HEADS * HD) ** -0.5, 0.15625, ((0, 4),))
    radius = touch_ends(jax.random.randint(streams_of[4], (HEADS,), 1, RMAX + 1), jax.random.fold_in(streams_of[4], 1), 1, RMAX).astype(jnp.int32)
    block_mask = draw_block_mask(jax.random.fold_in(streams_of[6], 71), 0)
    return {"query": query, "keys": keys, "values": values, "out_weight": out_weight, "radius": radius, "block_mask": block_mask}


def to_image(array, grid):
    width = array.shape[-1]
    array = array.reshape(NC, grid, grid, FRAMES, TH, TW, width)
    array = array.transpose(0, 3, 1, 4, 2, 5, 6)
    return array.reshape(NC, FRAMES, grid * TH, grid * TW, width)

def reference(query, keys, values, out_weight, radius, block_mask):
    grid = math.isqrt(N_TILE)
    high = grid * TH
    wide = grid * TW
    span = RMAX
    side = 2 * span + 1
    q_image = to_image(query, grid)
    pad_cfg = ((0, 0), (0, 0), (span, span), (span, span), (0, 0))
    k_image = jnp.pad(to_image(keys, grid), pad_cfg)
    v_image = jnp.pad(to_image(values, grid), pad_cfg)
    inside = jnp.pad(jnp.ones((high, wide), jnp.float32), span)
    shift_y = jnp.array(np.repeat(np.arange(-span, span + 1), side), dtype=jnp.int32)
    shift_x = jnp.array(np.tile(np.arange(-span, span + 1), side), dtype=jnp.int32)
    scale = 1.0 / math.sqrt(HD)

    def head_fn(head):
        q_head = lax.dynamic_slice_in_dim(q_image, head * HD, HD, 4).astype(jnp.float32)
        k_head = lax.dynamic_slice_in_dim(k_image, head * HD, HD, 4)
        v_head = lax.dynamic_slice_in_dim(v_image, head * HD, HD, 4)
        reach = radius[head]
        stretch_ok = (block_mask[head] > 0)[:, None, None, None, :, None]

        def score_at(index):
            step_y = shift_y[index]
            step_x = shift_x[index]
            zero = jnp.int32(0)
            starts = (zero, zero, (span + step_y).astype(jnp.int32), (span + step_x).astype(jnp.int32), zero)
            k_part = lax.dynamic_slice(k_head, starts, (NC, FRAMES, high, wide, HD)).astype(jnp.float32)
            v_part = lax.dynamic_slice(v_head, starts, (NC, FRAMES, high, wide, HD)).astype(jnp.float32)
            in_part = lax.dynamic_slice(inside, starts[2:4], (high, wide))
            scores = jnp.einsum('afyxd,bgyxd->afyxbg', q_head, k_part) * scale
            near = jnp.maximum(jnp.abs(step_y), jnp.abs(step_x)) <= reach
            usable = stretch_ok & (in_part[None, None, :, :, None, None] > 0) & near
            return (scores, usable, v_part)

        def top_step(index, best):
            scores, usable, v_part = score_at(index)
            masked = jnp.where(usable, scores, jnp.float32(-1e+30))
            return jnp.maximum(best, lax.optimization_barrier(jnp.max(masked, axis=(4, 5))))
        best = lax.fori_loop(0, side * side, top_step, jnp.full((NC, FRAMES, high, wide), -1e+30, jnp.float32))

        def add_step(index, carry):
            numer, denom = carry
            scores, usable, v_part = score_at(index)
            probs = jnp.where(usable, jnp.exp(scores - best[..., None, None]), jnp.float32(0.0))
            rounded = lax.optimization_barrier(probs.astype(jnp.bfloat16)).astype(jnp.float32)
            numer = numer + jnp.einsum('afyxbg,bgyxd->afyxd', rounded, v_part)
            denom = denom + lax.optimization_barrier(jnp.sum(probs, axis=(4, 5)))
            return (numer, denom)
        start = (jnp.zeros((NC, FRAMES, high, wide, HD), jnp.float32), jnp.zeros((NC, FRAMES, high, wide), jnp.float32))
        numer, denom = lax.fori_loop(0, side * side, add_step, start)
        return (numer / denom[..., None]).astype(jnp.bfloat16)
    attn = lax.map(head_fn, jnp.arange(HEADS, dtype=jnp.int32))
    attn = attn.transpose(1, 2, 3, 4, 0, 5).reshape(NC, FRAMES, grid, TH, grid, TW, HEADS * HD)
    attn = attn.transpose(0, 2, 4, 1, 3, 5, 6).reshape(NC * TILES * TOK, HEADS * HD)
    mixed = jnp.dot(attn, out_weight, preferred_element_type=jnp.float32).astype(jnp.bfloat16)
    return mixed.reshape(NC, TILES, TOK, D)
```

```python
import functools
import math

import jax
import jax.numpy as jnp
from jax import lax
from jax.experimental import pallas as pl
from jax.experimental.pallas import tpu as pltpu
from jax.sharding import PartitionSpec as P

MESH = pl.DeviceIdType.MESH
LOW = -1e30
STEPS = 6
ROWS = 272
LAG_UP = 1
LAG_END = 2


def attend(scale, q_ref, k_ref, v_ref, radius_ref, mask_ref, out_ref, *scratch):
    (kv, qb, pb, rb, ub, gb, ab, ar, bias, halo_s, halo_r, down_s, down_r, pair_s, pair_r,
     part_s, part_r, up_s, up_r, swap_s, swap_r) = scratch
    tm = lax.axis_index("tm")
    tile = lax.axis_index("tile")
    head = lax.axis_index("head")
    n_tm = lax.axis_size("tm")
    n_head = lax.axis_size("head")
    grid = math.isqrt(lax.axis_size("tile"))
    chips = n_tm // 2
    chip, core = tm // 2, tm % 2
    other = 1 - core
    row, col = tile // grid, tile % grid
    sibling = {"tm": chip * 2 + other}
    lower = {"tm": (tm + n_tm - 2) % n_tm}
    upper = {"tm": (tm + 2) % n_tm}

    def remote(src, dst, send, recv, device):
        return pltpu.make_async_remote_copy(
            src_ref=src, dst_ref=dst, send_sem=send, recv_sem=recv, device_id=device, device_id_type=MESH
        )

    sides = [(dy, dx) for dy in (-1, 0, 1) for dx in (-1, 0, 1) if (dy, dx) != (0, 0)]

    def on_grid(dy, dx):
        return (row + dy >= 0) & (row + dy < grid) & (col + dx >= 0) & (col + dx < grid)

    barrier = pltpu.get_barrier_semaphore()
    count = jnp.int32(2 + n_head)
    for device in (sibling, lower, upper):
        pl.semaphore_signal(barrier, inc=1, device_id=device, device_id_type=MESH)
    for off in range(1, n_head):
        pl.semaphore_signal(barrier, inc=1, device_id={"head": (head + off) % n_head}, device_id_type=MESH)
    for dy, dx in sides:
        count = count + on_grid(dy, dx).astype(jnp.int32)

        @pl.when(on_grid(dy, dx))
        def _():
            pl.semaphore_signal(barrier, inc=1, device_id={"tile": tile + dy * grid + dx}, device_id_type=MESH)

    for frame in (0, 1):
        for band in (0, 1):
            for pair in range(4):
                rows = q_ref[pl.ds(frame * 256 + (band * 8 + pair * 2) * 16, 32), :].astype(jnp.float32)
                for strip in (0, 1):
                    both = jnp.concatenate([rows[8 * strip : 8 * strip + 8], rows[16 + 8 * strip : 24 + 8 * strip]], axis=0)
                    both = both.astype(jnp.bfloat16)
                    for t in range(3):
                        qb[0, core, 2 * t + band, strip, pl.ds(frame * 64 + pair * 16, 16), :] = both[:, 128 * t : 128 * t + 128]

    top = lax.broadcasted_iota(jnp.int32, (8, 384), 0) < 4
    for which, ref in ((0, k_ref), (1, v_ref)):
        for frame in (0, 1):
            for by in range(4):
                rows = ref[pl.ds(frame * 256 + by * 64, 64), :].astype(jnp.float32)
                for bx in range(4):
                    start = 8 * (bx // 2)
                    halves = []
                    for y in (0, 2):
                        first = rows[16 * y + start : 16 * y + start + 8]
                        second = rows[16 * y + 16 + start : 16 * y + 24 + start]
                        if bx % 2 == 0:
                            halves.append(jnp.where(top, first, pltpu.roll(second, 4, 0)))
                        else:
                            halves.append(jnp.where(top, pltpu.roll(first, 4, 0), second))
                    block = jnp.concatenate(halves, axis=0).astype(jnp.bfloat16)
                    for t in range(3):
                        kv[which, t, 1 + by, 1 + bx, pl.ds(frame * 16, 16), :] = block[:, 128 * t : 128 * t + 128]

    pl.semaphore_wait(barrier, count)

    def down(kind, step):
        src, dst = ((0, 1), (1, 2), (0, 3))[kind]
        return remote(
            qb.at[src, core, step], qb.at[dst, core, step], down_s.at[kind, step], down_r.at[kind, step],
            upper if kind == 2 else lower,
        )

    def pair_of(d, step, slot):
        return remote(qb.at[d, slot, step], qb.at[d, slot, step], pair_s.at[d, step], pair_r.at[d, step], sibling)

    def part_of(d, step):
        return remote(pb.at[d, other, step], rb.at[d, step], part_s.at[d, step], part_r.at[d, step], sibling)

    def up(d, step):
        e = {2: 0, 1: 1, 3: 2}[d]
        return remote(
            ub.at[d - 1, step], gb.at[e, step], up_s.at[e, step], up_r.at[e, step], lower if d == 3 else upper
        )

    def halo(number):
        dy, dx = sides[number]
        src = {-1: slice(1, 2), 0: slice(1, 5), 1: slice(4, 5)}
        dst = {-1: slice(5, 6), 0: slice(1, 5), 1: slice(0, 1)}
        return remote(
            kv.at[:, :, src[dy], src[dx]], kv.at[:, :, dst[dy], dst[dx]], halo_s.at[number], halo_r.at[number],
            {"tile": (tile + dy * grid + dx) % (grid * grid)},
        )

    def swap(step, frame):
        return remote(
            ab.at[step, frame], ar.at[head, step // 2], swap_s.at[step, frame], swap_r.at[head, step // 2],
            {"head": frame * 2 + step % 2},
        )

    @pl.loop(0, STEPS)
    def _(step):
        @pl.when(chip >= 1)
        def _():
            down(0, step).start()

        @pl.when(chip == chips - 1)
        def _():
            down(2, step).start()

        @pl.when(core == 1)
        def _():
            pair_of(0, step, core).start()

    for number, (dy, dx) in enumerate(sides):
        @pl.when(on_grid(dy, dx))
        def _():
            halo(number).start()

    none = jnp.zeros((2, 3, 1, 6, 32, 128), jnp.bfloat16)
    for edge, at in ((row == 0, 0), (row == grid - 1, 5)):
        @pl.when(edge)
        def _():
            kv[:, :, at : at + 1, :] = none
    for edge, at in ((col == 0, 0), (col == grid - 1, 5)):
        @pl.when(edge)
        def _():
            kv[:, :, :, at : at + 1] = none.reshape(2, 3, 6, 1, 32, 128)

    def without(ref):
        @pl.loop(0, STEPS)
        def _(step):
            ref[step] = jnp.concatenate([jnp.zeros((256, 128), jnp.float32), jnp.full((16, 128), LOW, jnp.float32)], axis=0).astype(jnp.bfloat16)

    @pl.when(chip == 0)
    def _():
        without(gb.at[0])
        without(gb.at[1])

    @pl.when(chip != chips - 1)
    def _():
        without(gb.at[2])

    @pl.when(core == 0)
    def _():
        without(rb.at[0])

    query_at = lax.broadcasted_iota(jnp.int32, (128, 512), 0)
    key_at = lax.broadcasted_iota(jnp.int32, (128, 512), 1)
    query_y, query_x = (query_at >> 3) & 7, query_at & 7
    key_y = ((key_at >> 7) & 3) * 4 + ((key_at >> 2) & 3) - 4
    key_x = ((key_at >> 5) & 3) * 4 + (key_at & 3) - 4
    distance = jnp.maximum(jnp.abs(query_y - key_y), jnp.abs(query_x - key_x))

    @pl.loop(0, STEPS)
    def _(step):
        near = distance <= radius_ref[step // 2]
        at_y = row * 16 + (step % 2) * 8 + key_y
        for strip in (0, 1):
            at_x = col * 16 + strip * 8 + key_x
            inside = (at_y >= 0) & (at_y < grid * 16) & (at_x >= 0) & (at_x < grid * 16)
            bias[step, strip] = jnp.where(near & inside, jnp.float32(0.0), jnp.float32(LOW))

    for number, (dy, dx) in enumerate(sides):
        @pl.when(on_grid(-dy, -dx))
        def _():
            halo(number).wait_recv()

    lane = lax.broadcasted_iota(jnp.int32, (128, 128), 1)

    def unit(queries, step, strip):
        t, band = step // 2, step % 2
        k = kv[0, t, pl.ds(2 * band, 4), 2 * strip : 2 * strip + 4].reshape(512, 128)
        v = kv[1, t, pl.ds(2 * band, 4), 2 * strip : 2 * strip + 4].reshape(512, 128)
        slots = queries.shape[0] // 128
        s = lax.dot_general(queries, k, (((1,), (1,)), ((), ())), preferred_element_type=jnp.float32)
        s = s * scale
        allow = bias[step, strip]
        s = s + (allow if slots == 1 else jnp.concatenate([allow] * slots, axis=0))
        m = jnp.max(s, axis=1, keepdims=True)
        p = jnp.exp2(s - m).astype(jnp.bfloat16)
        wide = jnp.concatenate([v, jnp.ones((512, 128), jnp.bfloat16)], axis=1)
        o = jnp.dot(p, wide, preferred_element_type=jnp.float32)
        return o[:, :128], m, o[:, 128:]

    def put(ref, strips):
        for strip, (acc, m, l) in enumerate(strips):
            ref[pl.ds(strip * 128, 128), :] = acc.astype(jnp.bfloat16)
        (_, m0, l0), (_, m1, l1) = strips
        z = jnp.where(lane == 0, m0, jnp.where(lane == 1, l0, jnp.where(lane == 2, m1, jnp.where(lane == 3, l1, 0.0))))
        z = jnp.transpose(z)[:8]
        high = z.astype(jnp.bfloat16).astype(jnp.float32)
        rest = z - high
        mid = rest.astype(jnp.bfloat16).astype(jnp.float32)
        low = rest - mid
        ref[pl.ds(256, 16), :] = jnp.concatenate([high + pltpu.roll(mid, 4, 0), low], axis=0).astype(jnp.bfloat16)

    def get(ref):
        x = ref[pl.ds(256, 16), :].astype(jnp.float32)
        y = x[:8] + pltpu.roll(x[:8], 4, 0) + x[8:]
        y = jnp.transpose(jnp.concatenate([y] * 16, axis=0))
        return [(y[:, 2 * strip : 2 * strip + 1], y[:, 2 * strip + 1 : 2 * strip + 2]) for strip in (0, 1)]

    def merged(refs):
        sides_of = [get(ref) for ref in refs]
        result = []
        for strip in (0, 1):
            m = sides_of[0][strip][0]
            for one in sides_of[1:]:
                m = jnp.maximum(m, one[strip][0])
            acc, l = 0.0, 0.0
            for ref, one in zip(refs, sides_of):
                w = jnp.exp2(one[strip][0] - m)
                acc = acc + w * ref[pl.ds(strip * 128, 128), :].astype(jnp.float32)
                l = l + w * one[strip][1]
            result.append((acc, m, l))
        return result

    def masked(m, d, step, slot):
        visible = mask_ref[step // 2, 2 * (chip + d) + slot, tm]
        return jnp.where(visible > 0, m, jnp.float32(LOW))

    def alone(slot, step):
        strips = []
        for strip in (0, 1):
            acc, m, l = unit(qb[0, slot, step, strip], step, strip)
            strips.append((acc, masked(m, 0, step, slot), l))
        put(pb.at[0, slot, step], strips)

    def both(d, step):
        slots = ([], [])
        for strip in (0, 1):
            queries = qb[d, :, step, strip].reshape(256, 128)
            acc, m, l = unit(queries, step, strip)
            for slot in (0, 1):
                part = slice(128 * slot, 128 * slot + 128)
                slots[slot].append((acc[part], masked(m[part], d, step, slot), l[part]))
        for slot in (0, 1):
            put(pb.at[d, slot, step], slots[slot])

    def work(d, step):
        pair_of(d, step, other).wait_recv()
        both(d, step)
        part_of(d, step).start()

    def send_up(d, step):
        part_of(d, step).wait_recv()
        refs = [pb.at[d, core, step], rb.at[d, step]]
        if d == 1:
            @pl.when(chip >= 1)
            def _():
                up(2, step).wait_recv()

            refs.append(gb.at[0, step])
        put(ub.at[d - 1, step], merged(refs))
        up(d, step).start()

    def finish(step):
        @pl.when(core == 1)
        def _():
            part_of(0, step).wait_recv()

        @pl.when(chip >= 1)
        def _():
            up(1, step).wait_recv()

        @pl.when(chip == chips - 1)
        def _():
            up(3, step).wait_recv()

        strips = merged([pb.at[0, core, step], rb.at[0, step], gb.at[1, step], gb.at[2, step]])
        for strip, (acc, m, l) in enumerate(strips):
            attn = (acc / l).astype(jnp.bfloat16)
            for frame in (0, 1):
                ab[step, frame, strip] = attn[64 * frame : 64 * frame + 64]
        for frame in (0, 1):
            mine = head == frame * 2 + step % 2

            @pl.when(mine)
            def _():
                ar[head, step // 2] = ab[step, frame]

            @pl.when(jnp.logical_not(mine))
            def _():
                swap(step, frame).start()

    @pl.loop(0, STEPS)
    def _(step):
        alone(core, step)

        @pl.when(core == 0)
        def _():
            pair_of(0, step, other).wait_recv()
            alone(other, step)
            part_of(0, step).start()

    @pl.loop(0, STEPS + LAG_END)
    def _(i):
        @pl.when(i < STEPS)
        def _():
            @pl.when(chip < chips - 1)
            def _():
                down(0, i).wait_recv()

                @pl.when(chip >= 1)
                def _():
                    down(1, i).start()

                pair_of(1, i, core).start()

            @pl.when(chip == 0)
            def _():
                down(2, i).wait_recv()
                pair_of(3, i, core).start()

            @pl.when(chip < chips - 1)
            def _():
                work(1, i)

            @pl.when(chip == 0)
            def _():
                work(3, i)
                send_up(3, i)

            @pl.when(chip < chips - 2)
            def _():
                down(1, i).wait_recv()
                pair_of(2, i, core).start()
                work(2, i)
                send_up(2, i)

        @pl.when((i >= LAG_UP) & (i < STEPS + LAG_UP) & (chip < chips - 1))
        def _():
            send_up(1, i - LAG_UP)

        @pl.when(i >= LAG_END)
        def _():
            finish(i - LAG_END)

    for number, (dy, dx) in enumerate(sides):
        @pl.when(on_grid(dy, dx))
        def _():
            halo(number).wait_send()

    @pl.loop(0, STEPS)
    def _(step):
        @pl.when(chip >= 1)
        def _():
            down(0, step).wait_send()

        @pl.when((chip >= 1) & (chip < chips - 1))
        def _():
            down(1, step).wait_send()

        @pl.when(chip == chips - 1)
        def _():
            down(2, step).wait_send()

        @pl.when(core == 1)
        def _():
            pair_of(0, step, core).wait_send()

        @pl.when(core == 0)
        def _():
            part_of(0, step).wait_send()

        for d, there in ((1, chip < chips - 1), (2, chip < chips - 2), (3, chip == 0)):
            @pl.when(there)
            def _():
                pair_of(d, step, core).wait_send()
                part_of(d, step).wait_send()
                up(d, step).wait_send()

        for frame in (0, 1):
            @pl.when(head != frame * 2 + step % 2)
            def _():
                swap(step, frame).wait_send()

    for source in range(n_head):
        @pl.when(head != source)
        def _():
            for t in range(3):
                remote(
                    ab.at[0, 0], ar.at[source, t], swap_s.at[0, 0], swap_r.at[source, t],
                    {"head": (head + 1) % n_head},
                ).wait_recv()

    out_ref[...] = ar[...]


def project(a_ref, w_ref, o_ref):
    rows = jnp.concatenate([a_ref[z, t].reshape(128, 128) for z in range(4) for t in range(3)], axis=1)
    sums = jnp.dot(rows, w_ref[...], preferred_element_type=jnp.float32)
    pieces = []
    for y in range(8):
        for strip in (0, 1):
            pieces.append(sums[64 * strip + 8 * y : 64 * strip + 8 * y + 8])
    o_ref[...] = jnp.concatenate(pieces, axis=0).astype(jnp.bfloat16)


def per_device(query, keys, values, out_weight, radius, block_mask):
    width = out_weight.shape[1]
    scale = math.log2(math.e) / math.sqrt(128)
    weight = lax.all_gather(out_weight, "head", axis=0, tiled=True)
    vmem = pl.BlockSpec(memory_space=pltpu.VMEM)
    smem = pl.BlockSpec(memory_space=pltpu.SMEM)
    bf16 = jnp.bfloat16
    dma = pltpu.SemaphoreType.DMA
    attn = pl.pallas_call(
        functools.partial(attend, scale),
        out_shape=jax.ShapeDtypeStruct((4, 3, 2, 64, 128), bf16),
        in_specs=[vmem, vmem, vmem, smem, smem],
        out_specs=vmem,
        scratch_shapes=[
            pltpu.VMEM((2, 3, 6, 6, 32, 128), bf16),
            pltpu.VMEM((4, 2, STEPS, 2, 128, 128), bf16),
            pltpu.VMEM((4, 2, STEPS, ROWS, 128), bf16),
            pltpu.VMEM((4, STEPS, ROWS, 128), bf16),
            pltpu.VMEM((3, STEPS, ROWS, 128), bf16),
            pltpu.VMEM((3, STEPS, ROWS, 128), bf16),
            pltpu.VMEM((STEPS, 2, 2, 64, 128), bf16),
            pltpu.VMEM((4, 3, 2, 64, 128), bf16),
            pltpu.VMEM((STEPS, 2, 128, 512), jnp.float32),
            dma((8,)), dma((8,)),
            dma((3, STEPS)), dma((3, STEPS)),
            dma((4, STEPS)), dma((4, STEPS)),
            dma((4, STEPS)), dma((4, STEPS)),
            dma((3, STEPS)), dma((3, STEPS)),
            dma((STEPS, 2)), dma((4, 3)),
        ],
        compiler_params=pltpu.CompilerParams(
            collective_id=0, has_side_effects=True, vmem_limit_bytes=48 * 1024 * 1024
        ),
        cost_estimate=pl.CostEstimate(flops=6_400_000_000, bytes_accessed=2_000_000, transcendentals=6_000_000),
        name="attend",
    )(query.reshape(512, 384), keys.reshape(512, 384), values.reshape(512, 384), radius, block_mask)
    columns = 512
    mixed = pl.pallas_call(
        project,
        grid=(width // columns,),
        out_shape=jax.ShapeDtypeStruct((128, width), bf16),
        in_specs=[
            pl.BlockSpec((4, 3, 2, 64, 128), lambda i: (0, 0, 0, 0, 0)),
            pl.BlockSpec((1536, columns), lambda i: (0, i)),
        ],
        out_specs=pl.BlockSpec((128, columns), lambda i: (0, i)),
        compiler_params=pltpu.CompilerParams(vmem_limit_bytes=32 * 1024 * 1024),
        name="project",
    )(attn, weight)
    return mixed.reshape(1, 1, 128, width)


def solution(mesh):
    in_specs = (
        P("tm", "tile", None, None, None, "head"),
        P("tm", "tile", None, None, None, "head"),
        P("tm", "tile", None, None, None, "head"),
        P("head", None),
        P("head"),
        P("head", None, None),
    )
    out_specs = P("tm", "tile", "head", None)
    return jax.shard_map(per_device, mesh=mesh, in_specs=in_specs, out_specs=out_specs, check_vma=False)
```

```python
import functools
import math

import jax
import jax.numpy as jnp
from jax import lax
from jax.experimental import pallas as pl
from jax.experimental.pallas import tpu as pltpu
from jax.sharding import PartitionSpec as P

MESH = pl.DeviceIdType.MESH
LOW = -1e30
STEPS = 12
ROWS = 144
AHEAD = 2
LAG_END = 3


def attend(scale, q_in, k_in, v_in, w_in, radius_in, mask_in, out_ref, *scratch):
    (q_ref, k_ref, v_ref, radius_ref, mask_ref, kv, qb, pb, rb, ub, gb, ab, ar, bias, wf, total, load_s,
     halo_s, halo_r, down_s, down_r, pair_s, pair_r, part_s, part_r, up_s, up_r, swap_s, swap_r,
     weigh_s, weigh_r) = scratch
    tm = lax.axis_index("tm")
    tile = lax.axis_index("tile")
    head = lax.axis_index("head")
    n_tm = lax.axis_size("tm")
    n_head = lax.axis_size("head")
    grid = math.isqrt(lax.axis_size("tile"))
    chips = n_tm // 2
    chip, core = tm // 2, tm % 2
    other = 1 - core
    row, col = tile // grid, tile % grid
    sibling = {"tm": chip * 2 + other}

    def chip_off(d):
        return {"tm": (tm + 2 * d + n_tm) % n_tm}

    w_part = w_in.at[:, tile // 2, :, pl.ds(pl.multiple_of((2 * (tile % 2) + core) * 384, 384), 384)]
    loads = [
        pltpu.make_async_copy(src, dst, load_s.at[at])
        for at, (src, dst) in enumerate((
            (q_in, q_ref), (k_in, k_ref), (v_in, v_ref), (radius_in, radius_ref), (mask_in, mask_ref),
            (w_part, wf.at[core, tile, head]),
        ))
    ]
    for load in loads:
        load.start()

    def remote(src, dst, send, recv, device):
        return pltpu.make_async_remote_copy(
            src_ref=src, dst_ref=dst, send_sem=send, recv_sem=recv, device_id=device, device_id_type=MESH
        )

    sides = [(dy, dx) for dy in (-1, 0, 1) for dx in (-1, 0, 1) if (dy, dx) != (0, 0)]

    def on_grid(dy, dx):
        return (row + dy >= 0) & (row + dy < grid) & (col + dx >= 0) & (col + dx < grid)

    barrier = pltpu.get_barrier_semaphore()
    in_row = [{"tile": row * grid + (col + off) % grid} for off in range(1, grid)]
    in_col = [{"tile": (row + off) % grid * grid + col} for off in range(1, grid)]
    in_head = [{"head": (head + off) % n_head} for off in range(1, n_head)]
    always = [sibling] + [chip_off(d) for d in (1, 2, 3)] + in_row + in_col + in_head
    count = jnp.int32(len(always))
    for device in always:
        pl.semaphore_signal(barrier, inc=1, device_id=device, device_id_type=MESH)
    for dy, dx in sides:
        count = count + on_grid(dy, dx).astype(jnp.int32)

        @pl.when(on_grid(dy, dx))
        def _():
            pl.semaphore_signal(barrier, inc=1, device_id={"tile": tile + dy * grid + dx}, device_id_type=MESH)

    loads[0].wait()

    for frame in (0, 1):
        for band in (0, 1):
            for pair in range(4):
                rows = q_ref[pl.ds(frame * 256 + (band * 8 + pair * 2) * 16, 32), :].astype(jnp.float32)
                for strip in (0, 1):
                    both = jnp.concatenate([rows[8 * strip : 8 * strip + 8], rows[16 + 8 * strip : 24 + 8 * strip]], axis=0)
                    both = both.astype(jnp.bfloat16)
                    for t in range(3):
                        qb[0, core, 4 * t + 2 * band + strip, pl.ds(frame * 64 + pair * 16, 16), :] = both[:, 128 * t : 128 * t + 128]

    loads[1].wait()
    loads[2].wait()
    top = lax.broadcasted_iota(jnp.int32, (8, 384), 0) < 4
    for which, ref in ((0, k_ref), (1, v_ref)):
        for frame in (0, 1):
            for by in range(4):
                rows = ref[pl.ds(frame * 256 + by * 64, 64), :].astype(jnp.float32)
                for bx in range(4):
                    start = 8 * (bx // 2)
                    halves = []
                    for y in (0, 2):
                        first = rows[16 * y + start : 16 * y + start + 8]
                        second = rows[16 * y + 16 + start : 16 * y + 24 + start]
                        if bx % 2 == 0:
                            halves.append(jnp.where(top, first, pltpu.roll(second, 4, 0)))
                        else:
                            halves.append(jnp.where(top, pltpu.roll(first, 4, 0), second))
                    block = jnp.concatenate(halves, axis=0).astype(jnp.bfloat16)
                    for t in range(3):
                        kv[which, t, 1 + by, 1 + bx, pl.ds(frame * 16, 16), :] = block[:, 128 * t : 128 * t + 128]

    pl.semaphore_wait(barrier, count)

    def down(d, step):
        return remote(
            qb.at[0, core, step], qb.at[d, core, step], down_s.at[d - 1, step], down_r.at[d - 1, step], chip_off(-d)
        )

    def pair_of(d, step, slot):
        return remote(qb.at[d, slot, step], qb.at[d, slot, step], pair_s.at[d, step], pair_r.at[d, step], sibling)

    def part_of(d, step):
        return remote(pb.at[d, other, step], rb.at[d, step], part_s.at[d, step], part_r.at[d, step], sibling)

    def up(d, step):
        return remote(ub.at[d - 1, step], gb.at[d - 1, step], up_s.at[d - 1, step], up_r.at[d - 1, step], chip_off(d))

    def weigh(stage, at):
        mine = (
            wf.at[core, tile, head], wf.at[core, tile], wf.at[core, pl.ds(row * grid, grid)], wf.at[core],
        )[stage]
        to = (in_head, in_row, in_col, [sibling])[stage][at]
        return remote(mine, mine, weigh_s.at[stage, at], weigh_r.at[stage, at], to)

    def weigh_got(stage, at):
        off = at + 1
        there = (
            wf.at[core, tile, (head + n_head - off) % n_head],
            wf.at[core, row * grid + (col + grid - off) % grid],
            wf.at[core, pl.ds((row + grid - off) % grid * grid, grid)],
            wf.at[other],
        )[stage]
        to = (in_head, in_row, in_col, [sibling])[stage][at]
        return remote(there, there, weigh_s.at[stage, at], weigh_r.at[stage, at], to)

    stage_sizes = (n_head - 1, grid - 1, grid - 1, 1)

    def halo(number):
        dy, dx = sides[number]
        src = {-1: slice(1, 2), 0: slice(1, 5), 1: slice(4, 5)}
        dst = {-1: slice(5, 6), 0: slice(1, 5), 1: slice(0, 1)}
        return remote(
            kv.at[:, :, src[dy], src[dx]], kv.at[:, :, dst[dy], dst[dx]], halo_s.at[number], halo_r.at[number],
            {"tile": (tile + dy * grid + dx) % (grid * grid)},
        )

    def swap(step, frame):
        return remote(
            ab.at[step, frame], ar.at[head, step // 4, step % 2],
            swap_s.at[step, frame], swap_r.at[head, step // 4, step % 2], {"head": frame * 2 + step // 2 % 2},
        )

    def send_queries(step):
        for d in (1, 2, 3):
            @pl.when(chip >= d)
            def _():
                down(d, step).start()

    @pl.loop(0, AHEAD)
    def _(step):
        send_queries(step)

    @pl.when(core == 1)
    def _():
        @pl.loop(0, STEPS)
        def _(step):
            pair_of(0, step, core).start()

    for number, (dy, dx) in enumerate(sides):
        @pl.when(on_grid(dy, dx))
        def _():
            halo(number).start()

    loads[5].wait()
    for at in range(stage_sizes[0]):
        weigh(0, at).start()

    none = jnp.zeros((2, 3, 1, 6, 32, 128), jnp.bfloat16)
    for edge, at in ((row == 0, 0), (row == grid - 1, 5)):
        @pl.when(edge)
        def _():
            kv[:, :, at : at + 1, :] = none
    for edge, at in ((col == 0, 0), (col == grid - 1, 5)):
        @pl.when(edge)
        def _():
            kv[:, :, :, at : at + 1] = none.reshape(2, 3, 6, 1, 32, 128)

    def without(ref):
        @pl.loop(0, STEPS)
        def _(step):
            ref[step] = jnp.concatenate([jnp.zeros((128, 128), jnp.float32), jnp.full((16, 128), LOW, jnp.float32)], axis=0).astype(jnp.bfloat16)

    for d in (1, 2, 3):
        @pl.when(chip < d)
        def _():
            without(gb.at[d - 1])

    @pl.when(core == 0)
    def _():
        without(rb.at[0])

    loads[3].wait()
    loads[4].wait()
    query_at = lax.broadcasted_iota(jnp.int32, (128, 512), 0)
    key_at = lax.broadcasted_iota(jnp.int32, (128, 512), 1)
    query_y, query_x = (query_at >> 3) & 7, query_at & 7
    key_y = ((key_at >> 7) & 3) * 4 + ((key_at >> 2) & 3) - 4
    key_x = ((key_at >> 5) & 3) * 4 + (key_at & 3) - 4
    distance = jnp.maximum(jnp.abs(query_y - key_y), jnp.abs(query_x - key_x))

    @pl.loop(0, STEPS)
    def _(step):
        near = distance <= radius_ref[step // 4]
        at_y = row * 16 + (step // 2 % 2) * 8 + key_y
        at_x = col * 16 + (step % 2) * 8 + key_x
        inside = (at_y >= 0) & (at_y < grid * 16) & (at_x >= 0) & (at_x < grid * 16)
        bias[step] = jnp.where(near & inside, jnp.float32(0.0), jnp.float32(LOW))

    for number, (dy, dx) in enumerate(sides):
        @pl.when(on_grid(-dy, -dx))
        def _():
            halo(number).wait_recv()

    lane = lax.broadcasted_iota(jnp.int32, (128, 128), 1)

    def unit(queries, step):
        t, band, strip = step // 4, step // 2 % 2, step % 2
        k = kv[0, t, pl.ds(2 * band, 4), pl.ds(2 * strip, 4)].reshape(512, 128)
        v = kv[1, t, pl.ds(2 * band, 4), pl.ds(2 * strip, 4)].reshape(512, 128)
        slots = queries.shape[0] // 128
        s = lax.dot_general(queries, k, (((1,), (1,)), ((), ())), preferred_element_type=jnp.float32)
        s = s * scale
        allow = bias[step]
        s = s + (allow if slots == 1 else jnp.concatenate([allow] * slots, axis=0))
        m = jnp.max(s, axis=1, keepdims=True)
        p = jnp.exp2(s - m).astype(jnp.bfloat16)
        wide = jnp.concatenate([v, jnp.ones((512, 128), jnp.bfloat16)], axis=1)
        o = jnp.dot(p, wide, preferred_element_type=jnp.float32)
        return o[:, :128], m, o[:, 128:]

    def put(ref, acc, m, l):
        ref[pl.ds(0, 128), :] = acc.astype(jnp.bfloat16)
        z = jnp.transpose(jnp.where(lane == 0, m, jnp.where(lane == 1, l, 0.0)))[:8]
        high = z.astype(jnp.bfloat16).astype(jnp.float32)
        rest = z - high
        mid = rest.astype(jnp.bfloat16).astype(jnp.float32)
        low = rest - mid
        ref[pl.ds(128, 16), :] = jnp.concatenate([high + pltpu.roll(mid, 4, 0), low], axis=0).astype(jnp.bfloat16)

    def get(ref):
        x = ref[pl.ds(128, 16), :].astype(jnp.float32)
        y = x[:8] + pltpu.roll(x[:8], 4, 0) + x[8:]
        y = jnp.transpose(jnp.concatenate([y] * 16, axis=0))
        return y[:, 0:1], y[:, 1:2]

    def merged(refs):
        sides_of = [get(ref) for ref in refs]
        m = sides_of[0][0]
        for one in sides_of[1:]:
            m = jnp.maximum(m, one[0])
        acc, l = 0.0, 0.0
        for ref, one in zip(refs, sides_of):
            w = jnp.exp2(one[0] - m)
            acc = acc + w * ref[pl.ds(0, 128), :].astype(jnp.float32)
            l = l + w * one[1]
        return acc, m, l

    def masked(m, d, step, slot):
        visible = mask_ref[step // 4, 2 * (chip + d) + slot, tm]
        return jnp.where(visible > 0, m, jnp.float32(LOW))

    def alone(slot, step):
        acc, m, l = unit(qb[0, slot, step], step)
        put(pb.at[0, slot, step], acc, masked(m, 0, step, slot), l)

    def both(d, step):
        acc, m, l = unit(qb[d, :, step].reshape(256, 128), step)
        for slot in (0, 1):
            part = slice(128 * slot, 128 * slot + 128)
            put(pb.at[d, slot, step], acc[part], masked(m[part], d, step, slot), l[part])

    def work(d, step):
        pair_of(d, step, other).wait_recv()
        both(d, step)
        part_of(d, step).start()

    def send_up(d, step):
        part_of(d, step).wait_recv()
        put(ub.at[d - 1, step], *merged([pb.at[d, core, step], rb.at[d, step]]))
        up(d, step).start()

    def finish(step):
        @pl.when(core == 1)
        def _():
            part_of(0, step).wait_recv()

        for d in (1, 2, 3):
            @pl.when(chip >= d)
            def _():
                up(d, step).wait_recv()

        acc, _, l = merged([pb.at[0, core, step], rb.at[0, step]] + [gb.at[d - 1, step] for d in (1, 2, 3)])
        attn = (acc / l).astype(jnp.bfloat16)
        for frame in (0, 1):
            ab[step, frame] = attn[64 * frame : 64 * frame + 64]
        for frame in (0, 1):
            mine = head == frame * 2 + step // 2 % 2

            @pl.when(mine)
            def _():
                ar[head, step // 4, step % 2] = ab[step, frame]

            @pl.when(jnp.logical_not(mine))
            def _():
                swap(step, frame).start()

    @pl.loop(0, STEPS + LAG_END)
    def _(i):
        @pl.when(i < STEPS)
        def _():
            for d in (1, 2, 3):
                @pl.when(chip >= d)
                def _():
                    down(d, i).wait_send()

            @pl.when(i + AHEAD < STEPS)
            def _():
                send_queries(i + AHEAD)

            for d in (1, 2, 3):
                @pl.when(chip + d < chips)
                def _():
                    down(d, i).wait_recv()
                    pair_of(d, i, core).start()

            for d in (1, 2, 3):
                @pl.when(chip + d < chips)
                def _():
                    work(d, i)

            alone(core, i)

            @pl.when(core == 0)
            def _():
                pair_of(0, i, other).wait_recv()
                alone(other, i)
                part_of(0, i).start()

            for d in (1, 2, 3):
                @pl.when(chip + d < chips)
                def _():
                    send_up(d, i)

        for stage, when in ((0, 1), (1, 4), (2, 9)):
            @pl.when(i == when)
            def _():
                for at in range(stage_sizes[stage]):
                    weigh_got(stage, at).wait_recv()
                for at in range(stage_sizes[stage + 1]):
                    weigh(stage + 1, at).start()

        @pl.when(i >= LAG_END)
        def _():
            finish(i - LAG_END)

    weigh_got(3, 0).wait_recv()

    for t in range(3):
        for source in range(n_head):
            @pl.when(head != source)
            def _():
                for strip in (0, 1):
                    remote(
                        ab.at[0, 0], ar.at[source, t, strip], swap_s.at[0, 0], swap_r.at[source, t, strip],
                        {"head": (head + 1) % n_head},
                    ).wait_recv()

        rows = jnp.concatenate([ar[z, t].reshape(128, 128) for z in range(4)], axis=1)
        for part in range(4):
            at = slice(384 * part, 384 * part + 384)
            weight = jnp.concatenate(
                [wf[part % 2, 2 * group + part // 2, z, t] for z in range(4) for group in range(8)], axis=0
            )
            sums = jnp.dot(rows, weight, preferred_element_type=jnp.float32)
            if t > 0:
                sums = sums + total[:, at]
            if t < 2:
                total[:, at] = sums
            else:
                pieces = [
                    sums[64 * strip + 8 * y : 64 * strip + 8 * y + 8] for y in range(8) for strip in (0, 1)
                ]
                out_ref[:, at] = jnp.concatenate(pieces, axis=0).astype(jnp.bfloat16)

    for number, (dy, dx) in enumerate(sides):
        @pl.when(on_grid(dy, dx))
        def _():
            halo(number).wait_send()

    @pl.loop(0, STEPS)
    def _(step):
        @pl.when(core == 1)
        def _():
            pair_of(0, step, core).wait_send()

        @pl.when(core == 0)
        def _():
            part_of(0, step).wait_send()

        for d in (1, 2, 3):
            @pl.when(chip + d < chips)
            def _():
                pair_of(d, step, core).wait_send()
                part_of(d, step).wait_send()
                up(d, step).wait_send()

        for frame in (0, 1):
            @pl.when(head != frame * 2 + step // 2 % 2)
            def _():
                swap(step, frame).wait_send()

    for stage, size in enumerate(stage_sizes):
        for at in range(size):
            weigh(stage, at).wait_send()


def per_device(query, keys, values, out_weight, radius, block_mask):
    width = out_weight.shape[1]
    scale = math.log2(math.e) / math.sqrt(128)
    bf16 = jnp.bfloat16
    dma = pltpu.SemaphoreType.DMA
    mixed = pl.pallas_call(
        functools.partial(attend, scale),
        out_shape=jax.ShapeDtypeStruct((128, width), bf16),
        in_specs=[pl.BlockSpec(memory_space=pl.ANY)] * 6,
        out_specs=pl.BlockSpec(memory_space=pltpu.VMEM),
        scratch_shapes=[
            pltpu.VMEM((512, 384), bf16),
            pltpu.VMEM((512, 384), bf16),
            pltpu.VMEM((512, 384), bf16),
            pltpu.SMEM((3,), jnp.int32),
            pltpu.SMEM((3, 8, 8), jnp.int32),
            pltpu.VMEM((2, 3, 6, 6, 32, 128), bf16),
            pltpu.VMEM((4, 2, STEPS, 128, 128), bf16),
            pltpu.VMEM((4, 2, STEPS, ROWS, 128), bf16),
            pltpu.VMEM((4, STEPS, ROWS, 128), bf16),
            pltpu.VMEM((3, STEPS, ROWS, 128), bf16),
            pltpu.VMEM((3, STEPS, ROWS, 128), bf16),
            pltpu.VMEM((STEPS, 2, 64, 128), bf16),
            pltpu.VMEM((4, 3, 2, 64, 128), bf16),
            pltpu.VMEM((STEPS, 128, 512), jnp.float32),
            pltpu.VMEM((2, 16, 4, 3, 16, 384), bf16),
            pltpu.VMEM((128, width), jnp.float32),
            dma((6,)),
            dma((8,)), dma((8,)),
            dma((3, STEPS)), dma((3, STEPS)),
            dma((4, STEPS)), dma((4, STEPS)),
            dma((4, STEPS)), dma((4, STEPS)),
            dma((3, STEPS)), dma((3, STEPS)),
            dma((STEPS, 2)), dma((4, 3, 2)),
            dma((4, 3)), dma((4, 3)),
        ],
        compiler_params=pltpu.CompilerParams(
            collective_id=0, has_side_effects=True, vmem_limit_bytes=60 * 1024 * 1024
        ),
        cost_estimate=pl.CostEstimate(flops=6_400_000_000, bytes_accessed=2_000_000, transcendentals=6_000_000),
        name="attend",
    )(
        query.reshape(512, 384), keys.reshape(512, 384), values.reshape(512, 384),
        out_weight.reshape(3, 8, 16, width), radius, block_mask,
    )
    return mixed.reshape(1, 1, 128, width)


def solution(mesh):
    in_specs = (
        P("tm", "tile", None, None, None, "head"),
        P("tm", "tile", None, None, None, "head"),
        P("tm", "tile", None, None, None, "head"),
        P("head", None),
        P("head"),
        P("head", None, None),
    )
    out_specs = P("tm", "tile", "head", None)
    return jax.shard_map(per_device, mesh=mesh, in_specs=in_specs, out_specs=out_specs, check_vma=False)
```

```python
import functools
import math

import jax
import jax.numpy as jnp
from jax import lax
from jax.experimental import pallas as pl
from jax.experimental.pallas import tpu as pltpu
from jax.sharding import PartitionSpec as P

MESH = pl.DeviceIdType.MESH
LOW = -1e30
STEPS = 12
ROWS = 144
AHEAD = 2
LAG_END = 2


def attend(scale, q_in, k_in, v_in, w_in, radius_in, mask_in, out_ref, *scratch):
    (q_ref, k_ref, v_ref, radius_ref, mask_ref, kv, qb, pb, rb, ub, gb, ab, ar, bias, wf, total, load_s,
     halo_s, halo_r, down_s, down_r, pair_s, pair_r, part_s, part_r, up_s, up_r, swap_s, swap_r,
     weigh_s, weigh_r) = scratch
    tm = lax.axis_index("tm")
    tile = lax.axis_index("tile")
    head = lax.axis_index("head")
    n_tm = lax.axis_size("tm")
    n_head = lax.axis_size("head")
    grid = math.isqrt(lax.axis_size("tile"))
    chips = n_tm // 2
    chip, core = tm // 2, tm % 2
    other = 1 - core
    row, col = tile // grid, tile % grid
    sibling = {"tm": chip * 2 + other}

    def chip_off(d):
        return {"tm": (tm + 2 * d + n_tm) % n_tm}

    w_part = w_in.at[:, tile // 2, :, pl.ds(pl.multiple_of((2 * (tile % 2) + core) * 384, 384), 384)]
    loads = [
        pltpu.make_async_copy(src, dst, load_s.at[at])
        for at, (src, dst) in enumerate((
            (q_in, q_ref), (k_in, k_ref), (v_in, v_ref), (radius_in, radius_ref), (mask_in, mask_ref),
            (w_part, wf.at[core, tile, head]),
        ))
    ]
    for load in loads:
        load.start()

    def remote(src, dst, send, recv, device):
        return pltpu.make_async_remote_copy(
            src_ref=src, dst_ref=dst, send_sem=send, recv_sem=recv, device_id=device, device_id_type=MESH
        )

    sides = [(dy, dx) for dy in (-1, 0, 1) for dx in (-1, 0, 1) if (dy, dx) != (0, 0)]

    def on_grid(dy, dx):
        return (row + dy >= 0) & (row + dy < grid) & (col + dx >= 0) & (col + dx < grid)

    barrier = pltpu.get_barrier_semaphore()
    in_row = [{"tile": row * grid + (col + off) % grid} for off in range(1, grid)]
    in_col = [{"tile": (row + off) % grid * grid + col} for off in range(1, grid)]
    in_head = [{"head": (head + off) % n_head} for off in range(1, n_head)]
    always = [sibling] + [chip_off(d) for d in (1, 2, 3)] + in_row + in_col + in_head
    count = jnp.int32(len(always))
    for device in always:
        pl.semaphore_signal(barrier, inc=1, device_id=device, device_id_type=MESH)
    for dy, dx in sides:
        count = count + on_grid(dy, dx).astype(jnp.int32)

        @pl.when(on_grid(dy, dx))
        def _():
            pl.semaphore_signal(barrier, inc=1, device_id={"tile": tile + dy * grid + dx}, device_id_type=MESH)

    loads[0].wait()

    for frame in (0, 1):
        for band in (0, 1):
            for pair in range(4):
                rows = q_ref[pl.ds(frame * 256 + (band * 8 + pair * 2) * 16, 32), :].astype(jnp.float32)
                for strip in (0, 1):
                    both = jnp.concatenate([rows[8 * strip : 8 * strip + 8], rows[16 + 8 * strip : 24 + 8 * strip]], axis=0)
                    both = both.astype(jnp.bfloat16)
                    for t in range(3):
                        qb[0, core, 4 * t + 2 * band + strip, pl.ds(frame * 64 + pair * 16, 16), :] = both[:, 128 * t : 128 * t + 128]

    loads[1].wait()
    loads[2].wait()
    top = lax.broadcasted_iota(jnp.int32, (8, 384), 0) < 4
    for which, ref in ((0, k_ref), (1, v_ref)):
        for frame in (0, 1):
            for by in range(4):
                rows = ref[pl.ds(frame * 256 + by * 64, 64), :].astype(jnp.float32)
                for bx in range(4):
                    start = 8 * (bx // 2)
                    halves = []
                    for y in (0, 2):
                        first = rows[16 * y + start : 16 * y + start + 8]
                        second = rows[16 * y + 16 + start : 16 * y + 24 + start]
                        if bx % 2 == 0:
                            halves.append(jnp.where(top, first, pltpu.roll(second, 4, 0)))
                        else:
                            halves.append(jnp.where(top, pltpu.roll(first, 4, 0), second))
                    block = jnp.concatenate(halves, axis=0).astype(jnp.bfloat16)
                    for t in range(3):
                        kv[which, t, 1 + by, 1 + bx, pl.ds(frame * 16, 16), :] = block[:, 128 * t : 128 * t + 128]

    pl.semaphore_wait(barrier, count)

    def down(d, step):
        return remote(
            qb.at[0, core, step], qb.at[d, core, step], down_s.at[d - 1, step], down_r.at[d - 1, step], chip_off(-d)
        )

    def pair_of(d, step, slot):
        return remote(qb.at[d, slot, step], qb.at[d, slot, step], pair_s.at[d, step], pair_r.at[d, step], sibling)

    def part_of(d, step):
        return remote(pb.at[d, other, step], rb.at[d, step], part_s.at[d, step], part_r.at[d, step], sibling)

    def up(d, step):
        return remote(ub.at[d - 1, step], gb.at[d - 1, step], up_s.at[d - 1, step], up_r.at[d - 1, step], chip_off(d))

    def weigh(stage, at):
        mine = (
            wf.at[core, tile, head], wf.at[core, tile], wf.at[core, pl.ds(row * grid, grid)], wf.at[core],
        )[stage]
        to = (in_head, in_row, in_col, [sibling])[stage][at]
        return remote(mine, mine, weigh_s.at[stage, at], weigh_r.at[stage, at], to)

    def weigh_got(stage, at):
        off = at + 1
        there = (
            wf.at[core, tile, (head + n_head - off) % n_head],
            wf.at[core, row * grid + (col + grid - off) % grid],
            wf.at[core, pl.ds((row + grid - off) % grid * grid, grid)],
            wf.at[other],
        )[stage]
        to = (in_head, in_row, in_col, [sibling])[stage][at]
        return remote(there, there, weigh_s.at[stage, at], weigh_r.at[stage, at], to)

    stage_sizes = (n_head - 1, grid - 1, grid - 1, 1)

    def halo(number):
        dy, dx = sides[number]
        src = {-1: slice(1, 2), 0: slice(1, 5), 1: slice(4, 5)}
        dst = {-1: slice(5, 6), 0: slice(1, 5), 1: slice(0, 1)}
        return remote(
            kv.at[:, :, src[dy], src[dx]], kv.at[:, :, dst[dy], dst[dx]], halo_s.at[number], halo_r.at[number],
            {"tile": (tile + dy * grid + dx) % (grid * grid)},
        )

    def swap(step, frame):
        return remote(
            ab.at[step, frame], ar.at[head, step // 4, step % 2],
            swap_s.at[step, frame], swap_r.at[head, step // 4, step % 2], {"head": frame * 2 + step // 2 % 2},
        )

    def send_queries(step):
        for d in (1, 2, 3):
            @pl.when(chip >= d)
            def _():
                down(d, step).start()

    for number, (dy, dx) in enumerate(sides):
        @pl.when(on_grid(dy, dx))
        def _():
            halo(number).start()

    @pl.loop(0, AHEAD)
    def _(step):
        send_queries(step)

    @pl.when(core == 1)
    def _():
        @pl.loop(0, STEPS)
        def _(step):
            pair_of(0, step, core).start()

    loads[5].wait()
    for at in range(stage_sizes[0]):
        weigh(0, at).start()

    none = jnp.zeros((2, 3, 1, 6, 32, 128), jnp.bfloat16)
    for edge, at in ((row == 0, 0), (row == grid - 1, 5)):
        @pl.when(edge)
        def _():
            kv[:, :, at : at + 1, :] = none
    for edge, at in ((col == 0, 0), (col == grid - 1, 5)):
        @pl.when(edge)
        def _():
            kv[:, :, :, at : at + 1] = none.reshape(2, 3, 6, 1, 32, 128)

    def without(ref):
        @pl.loop(0, STEPS)
        def _(step):
            ref[step] = jnp.concatenate([jnp.zeros((128, 128), jnp.float32), jnp.full((16, 128), LOW, jnp.float32)], axis=0).astype(jnp.bfloat16)

    for d in (1, 2, 3):
        @pl.when(chip < d)
        def _():
            without(gb.at[d - 1])

    @pl.when(core == 0)
    def _():
        without(rb.at[0])

    loads[3].wait()
    loads[4].wait()
    query_at = lax.broadcasted_iota(jnp.int32, (128, 512), 0)
    key_at = lax.broadcasted_iota(jnp.int32, (128, 512), 1)
    query_y, query_x = (query_at >> 3) & 7, query_at & 7
    key_y = ((key_at >> 7) & 3) * 4 + ((key_at >> 2) & 3) - 4
    key_x = ((key_at >> 5) & 3) * 4 + (key_at & 3) - 4
    distance = jnp.maximum(jnp.abs(query_y - key_y), jnp.abs(query_x - key_x))

    @pl.loop(0, STEPS)
    def _(step):
        near = distance <= radius_ref[step // 4]
        at_y = row * 16 + (step // 2 % 2) * 8 + key_y
        at_x = col * 16 + (step % 2) * 8 + key_x
        inside = (at_y >= 0) & (at_y < grid * 16) & (at_x >= 0) & (at_x < grid * 16)
        bias[step] = jnp.where(near & inside, jnp.float32(0.0), jnp.float32(LOW))

    for number, (dy, dx) in enumerate(sides):
        @pl.when(on_grid(-dy, -dx))
        def _():
            halo(number).wait_recv()

    lane = lax.broadcasted_iota(jnp.int32, (128, 128), 1)

    def unit(queries, step):
        t, band, strip = step // 4, step // 2 % 2, step % 2
        k = kv[0, t, pl.ds(2 * band, 4), pl.ds(2 * strip, 4)].reshape(512, 128)
        v = kv[1, t, pl.ds(2 * band, 4), pl.ds(2 * strip, 4)].reshape(512, 128)
        slots = queries.shape[0] // 128
        s = lax.dot_general(queries, k, (((1,), (1,)), ((), ())), preferred_element_type=jnp.float32)
        s = s * scale
        allow = bias[step]
        s = s + (allow if slots == 1 else jnp.concatenate([allow] * slots, axis=0))
        m = jnp.max(s, axis=1, keepdims=True)
        p = jnp.exp2(s - m).astype(jnp.bfloat16)
        wide = jnp.concatenate([v, jnp.ones((512, 128), jnp.bfloat16)], axis=1)
        o = jnp.dot(p, wide, preferred_element_type=jnp.float32)
        return o[:, :128], m, o[:, 128:]

    def put(entries):
        z = jnp.zeros((128, 128), jnp.float32)
        for at, (ref, acc, m, l) in enumerate(entries):
            ref[pl.ds(0, 128), :] = acc.astype(jnp.bfloat16)
            z = jnp.where(lane == 8 * at, m, jnp.where(lane == 8 * at + 1, l, z))
        z = jnp.transpose(z)
        for at, (ref, _, _, _) in enumerate(entries):
            own = z[8 * at : 8 * at + 8]
            high = own.astype(jnp.bfloat16).astype(jnp.float32)
            rest = own - high
            mid = rest.astype(jnp.bfloat16).astype(jnp.float32)
            low = rest - mid
            ref[pl.ds(128, 16), :] = jnp.concatenate([high + pltpu.roll(mid, 4, 0), low], axis=0).astype(jnp.bfloat16)

    def merged(refs):
        packed = []
        for ref in refs:
            x = ref[pl.ds(128, 16), :].astype(jnp.float32)
            packed.append(x[:8] + pltpu.roll(x[:8], 4, 0) + x[8:])
        packed = jnp.concatenate(packed + [packed[0]] * (16 - len(refs)), axis=0)
        columns = jnp.transpose(packed)
        sides_of = [(columns[:, 8 * at : 8 * at + 1], columns[:, 8 * at + 1 : 8 * at + 2]) for at in range(len(refs))]
        m = sides_of[0][0]
        for one in sides_of[1:]:
            m = jnp.maximum(m, one[0])
        acc, l = 0.0, 0.0
        for ref, one in zip(refs, sides_of):
            w = jnp.exp2(one[0] - m)
            acc = acc + w * ref[pl.ds(0, 128), :].astype(jnp.float32)
            l = l + w * one[1]
        return acc, m, l

    def masked(m, d, step, slot):
        visible = mask_ref[step // 4, 2 * (chip + d) + slot, tm]
        return jnp.where(visible > 0, m, jnp.float32(LOW))

    def alone(slot, step):
        acc, m, l = unit(qb[0, slot, step], step)
        put([(pb.at[0, slot, step], acc, masked(m, 0, step, slot), l)])

    def both(d, step):
        acc, m, l = unit(qb[d, :, step].reshape(256, 128), step)
        entries = []
        for slot in (0, 1):
            part = slice(128 * slot, 128 * slot + 128)
            entries.append((pb.at[d, slot, step], acc[part], masked(m[part], d, step, slot), l[part]))
        put(entries)

    def work(d, step):
        pair_of(d, step, other).wait_recv()
        both(d, step)
        part_of(d, step).start()

    def send_up(d, step):
        part_of(d, step).wait_recv()
        put([(ub.at[d - 1, step], *merged([pb.at[d, core, step], rb.at[d, step]]))])
        up(d, step).start()

    def finish(step):
        @pl.when(core == 1)
        def _():
            part_of(0, step).wait_recv()

        for d in (1, 2, 3):
            @pl.when(chip >= d)
            def _():
                up(d, step).wait_recv()

        acc, _, l = merged([pb.at[0, core, step], rb.at[0, step]] + [gb.at[d - 1, step] for d in (1, 2, 3)])
        attn = (acc / l).astype(jnp.bfloat16)
        for frame in (0, 1):
            ab[step, frame] = attn[64 * frame : 64 * frame + 64]
        for frame in (0, 1):
            mine = head == frame * 2 + step // 2 % 2

            @pl.when(mine)
            def _():
                ar[head, step // 4, step % 2] = ab[step, frame]

            @pl.when(jnp.logical_not(mine))
            def _():
                swap(step, frame).start()

    @pl.loop(0, STEPS + LAG_END)
    def _(i):
        @pl.when(i < STEPS)
        def _():
            for d in (1, 2, 3):
                @pl.when(chip >= d)
                def _():
                    down(d, i).wait_send()

            for d in (1, 2, 3):
                @pl.when(chip + d < chips)
                def _():
                    down(d, i).wait_recv()
                    pair_of(d, i, core).start()

            @pl.when(i + AHEAD < STEPS)
            def _():
                send_queries(i + AHEAD)

            for d in (1, 2, 3):
                @pl.when(chip + d < chips)
                def _():
                    work(d, i)

            @pl.when(core == 1)
            def _():
                alone(core, i)

            @pl.when(core == 0)
            def _():
                pair_of(0, i, other).wait_recv()
                both(0, i)
                part_of(0, i).start()

            for d in (1, 2, 3):
                @pl.when(chip + d < chips)
                def _():
                    send_up(d, i)

        for stage, when in ((0, 1), (1, 4), (2, 9)):
            @pl.when(i == when)
            def _():
                for at in range(stage_sizes[stage]):
                    weigh_got(stage, at).wait_recv()
                for at in range(stage_sizes[stage + 1]):
                    weigh(stage + 1, at).start()

        @pl.when(i >= LAG_END)
        def _():
            finish(i - LAG_END)

    weigh_got(3, 0).wait_recv()

    for t in range(3):
        for source in range(n_head):
            @pl.when(head != source)
            def _():
                for strip in (0, 1):
                    remote(
                        ab.at[0, 0], ar.at[source, t, strip], swap_s.at[0, 0], swap_r.at[source, t, strip],
                        {"head": (head + 1) % n_head},
                    ).wait_recv()

        rows = jnp.concatenate([ar[z, t].reshape(128, 128) for z in range(4)], axis=1)
        for part in range(4):
            at = slice(384 * part, 384 * part + 384)
            weight = jnp.concatenate(
                [wf[part % 2, 2 * group + part // 2, z, t] for z in range(4) for group in range(8)], axis=0
            )
            sums = jnp.dot(rows, weight, preferred_element_type=jnp.float32)
            if t > 0:
                sums = sums + total[:, at]
            if t < 2:
                total[:, at] = sums
            else:
                pieces = [
                    sums[64 * strip + 8 * y : 64 * strip + 8 * y + 8] for y in range(8) for strip in (0, 1)
                ]
                out_ref[:, at] = jnp.concatenate(pieces, axis=0).astype(jnp.bfloat16)

    for number, (dy, dx) in enumerate(sides):
        @pl.when(on_grid(dy, dx))
        def _():
            halo(number).wait_send()

    @pl.loop(0, STEPS)
    def _(step):
        @pl.when(core == 1)
        def _():
            pair_of(0, step, core).wait_send()

        @pl.when(core == 0)
        def _():
            part_of(0, step).wait_send()

        for d in (1, 2, 3):
            @pl.when(chip + d < chips)
            def _():
                pair_of(d, step, core).wait_send()
                part_of(d, step).wait_send()
                up(d, step).wait_send()

        for frame in (0, 1):
            @pl.when(head != frame * 2 + step // 2 % 2)
            def _():
                swap(step, frame).wait_send()

    for stage, size in enumerate(stage_sizes):
        for at in range(size):
            weigh(stage, at).wait_send()


def per_device(query, keys, values, out_weight, radius, block_mask):
    width = out_weight.shape[1]
    scale = math.log2(math.e) / math.sqrt(128)
    bf16 = jnp.bfloat16
    dma = pltpu.SemaphoreType.DMA
    mixed = pl.pallas_call(
        functools.partial(attend, scale),
        out_shape=jax.ShapeDtypeStruct((128, width), bf16),
        in_specs=[pl.BlockSpec(memory_space=pl.ANY)] * 6,
        out_specs=pl.BlockSpec(memory_space=pltpu.VMEM),
        scratch_shapes=[
            pltpu.VMEM((512, 384), bf16),
            pltpu.VMEM((512, 384), bf16),
            pltpu.VMEM((512, 384), bf16),
            pltpu.SMEM((3,), jnp.int32),
            pltpu.SMEM((3, 8, 8), jnp.int32),
            pltpu.VMEM((2, 3, 6, 6, 32, 128), bf16),
            pltpu.VMEM((4, 2, STEPS, 128, 128), bf16),
            pltpu.VMEM((4, 2, STEPS, ROWS, 128), bf16),
            pltpu.VMEM((4, STEPS, ROWS, 128), bf16),
            pltpu.VMEM((3, STEPS, ROWS, 128), bf16),
            pltpu.VMEM((3, STEPS, ROWS, 128), bf16),
            pltpu.VMEM((STEPS, 2, 64, 128), bf16),
            pltpu.VMEM((4, 3, 2, 64, 128), bf16),
            pltpu.VMEM((STEPS, 128, 512), jnp.float32),
            pltpu.VMEM((2, 16, 4, 3, 16, 384), bf16),
            pltpu.VMEM((128, width), jnp.float32),
            dma((6,)),
            dma((8,)), dma((8,)),
            dma((3, STEPS)), dma((3, STEPS)),
            dma((4, STEPS)), dma((4, STEPS)),
            dma((4, STEPS)), dma((4, STEPS)),
            dma((3, STEPS)), dma((3, STEPS)),
            dma((STEPS, 2)), dma((4, 3, 2)),
            dma((4, 3)), dma((4, 3)),
        ],
        compiler_params=pltpu.CompilerParams(
            collective_id=0, has_side_effects=True, vmem_limit_bytes=60 * 1024 * 1024
        ),
        cost_estimate=pl.CostEstimate(flops=6_400_000_000, bytes_accessed=2_000_000, transcendentals=6_000_000),
        name="attend",
    )(
        query.reshape(512, 384), keys.reshape(512, 384), values.reshape(512, 384),
        out_weight.reshape(3, 8, 16, width), radius, block_mask,
    )
    return mixed.reshape(1, 1, 128, width)


def solution(mesh):
    in_specs = (
        P("tm", "tile", None, None, None, "head"),
        P("tm", "tile", None, None, None, "head"),
        P("tm", "tile", None, None, None, "head"),
        P("head", None),
        P("head"),
        P("head", None, None),
    )
    out_specs = P("tm", "tile", "head", None)
    return jax.shard_map(per_device, mesh=mesh, in_specs=in_specs, out_specs=out_specs, check_vma=False)
```

```python
import functools
import math

import jax
import jax.numpy as jnp
from jax import lax
from jax.experimental import pallas as pl
from jax.experimental.pallas import tpu as pltpu
from jax.sharding import PartitionSpec as P

MESH = pl.DeviceIdType.MESH
LOW = -1e30
STEPS = 12
ROWS = 144
AHEAD = 2
LAG_END = 2


def attend(scale, q_in, k_in, v_in, w_in, radius_in, mask_in, out_ref, *scratch):
    (q_ref, k_ref, v_ref, radius_ref, mask_ref, kv, qb, pb, rb, ub, gb, ab, ar, bias, wf, total, load_s,
     halo_s, halo_r, down_s, down_r, pair_s, pair_r, part_s, part_r, up_s, up_r, swap_s, swap_r,
     weigh_s, weigh_r) = scratch
    tm = lax.axis_index("tm")
    tile = lax.axis_index("tile")
    head = lax.axis_index("head")
    n_tm = lax.axis_size("tm")
    n_head = lax.axis_size("head")
    grid = math.isqrt(lax.axis_size("tile"))
    chips = n_tm // 2
    chip, core = tm // 2, tm % 2
    other = 1 - core
    row, col = tile // grid, tile % grid
    sibling = {"tm": chip * 2 + other}

    def chip_off(d):
        return {"tm": (tm + 2 * d + n_tm) % n_tm}

    w_part = w_in.at[:, tile // 2, :, pl.ds(pl.multiple_of((2 * (tile % 2) + core) * 384, 384), 384)]
    loads = [
        pltpu.make_async_copy(src, dst, load_s.at[at])
        for at, (src, dst) in enumerate((
            (q_in, q_ref), (k_in, k_ref), (v_in, v_ref), (radius_in, radius_ref), (mask_in, mask_ref),
            (w_part, wf.at[core, tile, head]),
        ))
    ]
    for load in loads:
        load.start()

    def remote(src, dst, send, recv, device):
        return pltpu.make_async_remote_copy(
            src_ref=src, dst_ref=dst, send_sem=send, recv_sem=recv, device_id=device, device_id_type=MESH
        )

    sides = [(dy, dx) for dy in (-1, 0, 1) for dx in (-1, 0, 1) if (dy, dx) != (0, 0)]

    def on_grid(dy, dx):
        return (row + dy >= 0) & (row + dy < grid) & (col + dx >= 0) & (col + dx < grid)

    barrier = pltpu.get_barrier_semaphore()
    in_row = [{"tile": row * grid + (col + off) % grid} for off in range(1, grid)]
    in_col = [{"tile": (row + off) % grid * grid + col} for off in range(1, grid)]
    in_head = [{"head": (head + off) % n_head} for off in range(1, n_head)]
    always = [sibling] + [chip_off(d) for d in (1, 2, 3)] + in_row + in_col + in_head
    count = jnp.int32(len(always))
    for device in always:
        pl.semaphore_signal(barrier, inc=1, device_id=device, device_id_type=MESH)
    for dy, dx in sides:
        count = count + on_grid(dy, dx).astype(jnp.int32)

        @pl.when(on_grid(dy, dx))
        def _():
            pl.semaphore_signal(barrier, inc=1, device_id={"tile": tile + dy * grid + dx}, device_id_type=MESH)

    loads[0].wait()

    for frame in (0, 1):
        for band in (0, 1):
            for pair in range(4):
                rows = q_ref[pl.ds(frame * 256 + (band * 8 + pair * 2) * 16, 32), :].astype(jnp.float32)
                for strip in (0, 1):
                    both = jnp.concatenate([rows[8 * strip : 8 * strip + 8], rows[16 + 8 * strip : 24 + 8 * strip]], axis=0)
                    both = both.astype(jnp.bfloat16)
                    for t in range(3):
                        qb[0, core, 4 * t + 2 * band + strip, pl.ds(frame * 64 + pair * 16, 16), :] = both[:, 128 * t : 128 * t + 128]

    loads[1].wait()
    loads[2].wait()
    top = lax.broadcasted_iota(jnp.int32, (8, 384), 0) < 4
    for which, ref in ((0, k_ref), (1, v_ref)):
        for frame in (0, 1):
            for by in range(4):
                rows = ref[pl.ds(frame * 256 + by * 64, 64), :].astype(jnp.float32)
                for bx in range(4):
                    start = 8 * (bx // 2)
                    halves = []
                    for y in (0, 2):
                        first = rows[16 * y + start : 16 * y + start + 8]
                        second = rows[16 * y + 16 + start : 16 * y + 24 + start]
                        if bx % 2 == 0:
                            halves.append(jnp.where(top, first, pltpu.roll(second, 4, 0)))
                        else:
                            halves.append(jnp.where(top, pltpu.roll(first, 4, 0), second))
                    block = jnp.concatenate(halves, axis=0).astype(jnp.bfloat16)
                    for t in range(3):
                        kv[which, t, 1 + by, 1 + bx, pl.ds(frame * 16, 16), :] = block[:, 128 * t : 128 * t + 128]

    pl.semaphore_wait(barrier, count)

    def down(d, step):
        return remote(
            qb.at[0, core, step], qb.at[d, core, step], down_s.at[d - 1, step], down_r.at[d - 1, step], chip_off(-d)
        )

    def pair_of(d, step, slot):
        return remote(qb.at[d, slot, step], qb.at[d, slot, step], pair_s.at[d, step], pair_r.at[d, step], sibling)

    def part_of(d, step):
        return remote(pb.at[d, other, step], rb.at[d, step], part_s.at[d, step], part_r.at[d, step], sibling)

    def up(d, step):
        return remote(ub.at[d - 1, step], gb.at[d - 1, step], up_s.at[d - 1, step], up_r.at[d - 1, step], chip_off(d))

    def weigh(stage, at):
        mine = (
            wf.at[core, tile, head], wf.at[core, tile], wf.at[core, pl.ds(row * grid, grid)], wf.at[core],
        )[stage]
        to = (in_head, in_row, in_col, [sibling])[stage][at]
        return remote(mine, mine, weigh_s.at[stage, at], weigh_r.at[stage, at], to)

    def weigh_got(stage, at):
        off = at + 1
        there = (
            wf.at[core, tile, (head + n_head - off) % n_head],
            wf.at[core, row * grid + (col + grid - off) % grid],
            wf.at[core, pl.ds((row + grid - off) % grid * grid, grid)],
            wf.at[other],
        )[stage]
        to = (in_head, in_row, in_col, [sibling])[stage][at]
        return remote(there, there, weigh_s.at[stage, at], weigh_r.at[stage, at], to)

    stage_sizes = (n_head - 1, grid - 1, grid - 1, 1)

    def halo(number):
        dy, dx = sides[number]
        src = {-1: slice(1, 2), 0: slice(1, 5), 1: slice(4, 5)}
        dst = {-1: slice(5, 6), 0: slice(1, 5), 1: slice(0, 1)}
        return remote(
            kv.at[:, :, src[dy], src[dx]], kv.at[:, :, dst[dy], dst[dx]], halo_s.at[number], halo_r.at[number],
            {"tile": (tile + dy * grid + dx) % (grid * grid)},
        )

    def swap(step, frame):
        return remote(
            ab.at[step, frame], ar.at[head, step // 4, step % 2],
            swap_s.at[step, frame], swap_r.at[head, step // 4, step % 2], {"head": frame * 2 + step // 2 % 2},
        )

    def relay(step):
        return remote(
            qb.at[3, core, step], qb.at[2, core, step], down_s.at[1, step], down_r.at[1, step], chip_off(1)
        )

    def sends(d):
        return chip == d if d == 2 else chip >= d

    def send_queries(step):
        for d in (1, 2, 3):
            @pl.when(sends(d))
            def _():
                down(d, step).start()

    for number, (dy, dx) in enumerate(sides):
        @pl.when(on_grid(dy, dx))
        def _():
            halo(number).start()

    @pl.loop(0, AHEAD)
    def _(step):
        send_queries(step)

    @pl.when(core == 1)
    def _():
        @pl.loop(0, STEPS)
        def _(step):
            pair_of(0, step, core).start()

    loads[5].wait()
    for at in range(stage_sizes[0]):
        weigh(0, at).start()

    none = jnp.zeros((2, 3, 1, 6, 32, 128), jnp.bfloat16)
    for edge, at in ((row == 0, 0), (row == grid - 1, 5)):
        @pl.when(edge)
        def _():
            kv[:, :, at : at + 1, :] = none
    for edge, at in ((col == 0, 0), (col == grid - 1, 5)):
        @pl.when(edge)
        def _():
            kv[:, :, :, at : at + 1] = none.reshape(2, 3, 6, 1, 32, 128)

    def without(ref):
        @pl.loop(0, STEPS)
        def _(step):
            ref[step] = jnp.concatenate([jnp.zeros((128, 128), jnp.float32), jnp.full((16, 128), LOW, jnp.float32)], axis=0).astype(jnp.bfloat16)

    for d in (1, 2, 3):
        @pl.when(chip < d)
        def _():
            without(gb.at[d - 1])

    @pl.when(core == 0)
    def _():
        without(rb.at[0])

    loads[3].wait()
    loads[4].wait()
    query_at = lax.broadcasted_iota(jnp.int32, (128, 512), 0)
    key_at = lax.broadcasted_iota(jnp.int32, (128, 512), 1)
    query_y, query_x = (query_at >> 3) & 7, query_at & 7
    key_y = ((key_at >> 7) & 3) * 4 + ((key_at >> 2) & 3) - 4
    key_x = ((key_at >> 5) & 3) * 4 + (key_at & 3) - 4
    distance = jnp.maximum(jnp.abs(query_y - key_y), jnp.abs(query_x - key_x))

    @pl.loop(0, STEPS)
    def _(step):
        near = distance <= radius_ref[step // 4]
        at_y = row * 16 + (step // 2 % 2) * 8 + key_y
        at_x = col * 16 + (step % 2) * 8 + key_x
        inside = (at_y >= 0) & (at_y < grid * 16) & (at_x >= 0) & (at_x < grid * 16)
        bias[step] = jnp.where(near & inside, jnp.float32(0.0), jnp.float32(LOW))

    for number, (dy, dx) in enumerate(sides):
        @pl.when(on_grid(-dy, -dx))
        def _():
            halo(number).wait_recv()

    lane = lax.broadcasted_iota(jnp.int32, (128, 128), 1)

    def unit(queries, step):
        t, band, strip = step // 4, step // 2 % 2, step % 2
        k = kv[0, t, pl.ds(2 * band, 4), pl.ds(2 * strip, 4)].reshape(512, 128)
        v = kv[1, t, pl.ds(2 * band, 4), pl.ds(2 * strip, 4)].reshape(512, 128)
        slots = queries.shape[0] // 128
        s = lax.dot_general(queries, k, (((1,), (1,)), ((), ())), preferred_element_type=jnp.float32)
        s = s * scale
        allow = bias[step]
        s = s + (allow if slots == 1 else jnp.concatenate([allow] * slots, axis=0))
        m = jnp.max(s, axis=1, keepdims=True)
        p = jnp.exp2(s - m).astype(jnp.bfloat16)
        wide = jnp.concatenate([v, jnp.ones((512, 128), jnp.bfloat16)], axis=1)
        o = jnp.dot(p, wide, preferred_element_type=jnp.float32)
        return o[:, :128], m, o[:, 128:]

    def put(entries):
        z = jnp.zeros((128, 128), jnp.float32)
        for at, (ref, acc, m, l) in enumerate(entries):
            ref[pl.ds(0, 128), :] = acc.astype(jnp.bfloat16)
            z = jnp.where(lane == 8 * at, m, jnp.where(lane == 8 * at + 1, l, z))
        z = jnp.transpose(z)
        for at, (ref, _, _, _) in enumerate(entries):
            own = z[8 * at : 8 * at + 8]
            high = own.astype(jnp.bfloat16).astype(jnp.float32)
            rest = own - high
            mid = rest.astype(jnp.bfloat16).astype(jnp.float32)
            low = rest - mid
            ref[pl.ds(128, 16), :] = jnp.concatenate([high + pltpu.roll(mid, 4, 0), low], axis=0).astype(jnp.bfloat16)

    def merged(refs):
        packed = []
        for ref in refs:
            x = ref[pl.ds(128, 16), :].astype(jnp.float32)
            packed.append(x[:8] + pltpu.roll(x[:8], 4, 0) + x[8:])
        packed = jnp.concatenate(packed + [packed[0]] * (16 - len(refs)), axis=0)
        columns = jnp.transpose(packed)
        sides_of = [(columns[:, 8 * at : 8 * at + 1], columns[:, 8 * at + 1 : 8 * at + 2]) for at in range(len(refs))]
        m = sides_of[0][0]
        for one in sides_of[1:]:
            m = jnp.maximum(m, one[0])
        acc, l = 0.0, 0.0
        for ref, one in zip(refs, sides_of):
            w = jnp.exp2(one[0] - m)
            acc = acc + w * ref[pl.ds(0, 128), :].astype(jnp.float32)
            l = l + w * one[1]
        return acc, m, l

    def masked(m, d, step, slot):
        visible = mask_ref[step // 4, 2 * (chip + d) + slot, tm]
        return jnp.where(visible > 0, m, jnp.float32(LOW))

    def alone(slot, step):
        acc, m, l = unit(qb[0, slot, step], step)
        put([(pb.at[0, slot, step], acc, masked(m, 0, step, slot), l)])

    def both(d, step):
        acc, m, l = unit(qb[d, :, step].reshape(256, 128), step)
        entries = []
        for slot in (0, 1):
            part = slice(128 * slot, 128 * slot + 128)
            entries.append((pb.at[d, slot, step], acc[part], masked(m[part], d, step, slot), l[part]))
        put(entries)

    def work(d, step):
        pair_of(d, step, other).wait_recv()
        both(d, step)
        part_of(d, step).start()

    def send_up(d, step):
        part_of(d, step).wait_recv()
        put([(ub.at[d - 1, step], *merged([pb.at[d, core, step], rb.at[d, step]]))])
        up(d, step).start()

    def finish(step):
        @pl.when(core == 1)
        def _():
            part_of(0, step).wait_recv()

        for d in (1, 2, 3):
            @pl.when(chip >= d)
            def _():
                up(d, step).wait_recv()

        acc, _, l = merged([pb.at[0, core, step], rb.at[0, step]] + [gb.at[d - 1, step] for d in (1, 2, 3)])
        attn = (acc / l).astype(jnp.bfloat16)
        for frame in (0, 1):
            ab[step, frame] = attn[64 * frame : 64 * frame + 64]
        for frame in (0, 1):
            mine = head == frame * 2 + step // 2 % 2

            @pl.when(mine)
            def _():
                ar[head, step // 4, step % 2] = ab[step, frame]

            @pl.when(jnp.logical_not(mine))
            def _():
                swap(step, frame).start()

    @pl.loop(0, STEPS + LAG_END)
    def _(i):
        @pl.when(i < STEPS)
        def _():
            for d in (1, 2, 3):
                @pl.when(sends(d))
                def _():
                    down(d, i).wait_send()

            @pl.when(i + AHEAD < STEPS)
            def _():
                send_queries(i + AHEAD)

            for d in (3, 1, 2):
                @pl.when(chip + d < chips)
                def _():
                    down(d, i).wait_recv()
                    if d == 3:
                        relay(i).start()
                    pair_of(d, i, core).start()

            for d in (1, 2, 3):
                @pl.when(chip + d < chips)
                def _():
                    work(d, i)

            @pl.when(core == 1)
            def _():
                alone(core, i)

            @pl.when(core == 0)
            def _():
                pair_of(0, i, other).wait_recv()
                both(0, i)
                part_of(0, i).start()

            for d in (1, 2, 3):
                @pl.when(chip + d < chips)
                def _():
                    send_up(d, i)

        for stage, when in ((0, 1), (1, 4), (2, 9)):
            @pl.when(i == when)
            def _():
                for at in range(stage_sizes[stage]):
                    weigh_got(stage, at).wait_recv()
                for at in range(stage_sizes[stage + 1]):
                    weigh(stage + 1, at).start()

        @pl.when(i >= LAG_END)
        def _():
            finish(i - LAG_END)

    weigh_got(3, 0).wait_recv()

    for t in range(3):
        for source in range(n_head):
            @pl.when(head != source)
            def _():
                for strip in (0, 1):
                    remote(
                        ab.at[0, 0], ar.at[source, t, strip], swap_s.at[0, 0], swap_r.at[source, t, strip],
                        {"head": (head + 1) % n_head},
                    ).wait_recv()

        rows = jnp.concatenate([ar[z, t].reshape(128, 128) for z in range(4)], axis=1)
        for part in range(4):
            at = slice(384 * part, 384 * part + 384)
            weight = jnp.concatenate(
                [wf[part % 2, 2 * group + part // 2, z, t] for z in range(4) for group in range(8)], axis=0
            )
            sums = jnp.dot(rows, weight, preferred_element_type=jnp.float32)
            if t > 0:
                sums = sums + total[:, at]
            if t < 2:
                total[:, at] = sums
            else:
                pieces = [
                    sums[64 * strip + 8 * y : 64 * strip + 8 * y + 8] for y in range(8) for strip in (0, 1)
                ]
                out_ref[:, at] = jnp.concatenate(pieces, axis=0).astype(jnp.bfloat16)

    for number, (dy, dx) in enumerate(sides):
        @pl.when(on_grid(dy, dx))
        def _():
            halo(number).wait_send()

    @pl.loop(0, STEPS)
    def _(step):
        @pl.when(core == 1)
        def _():
            pair_of(0, step, core).wait_send()

        @pl.when(core == 0)
        def _():
            part_of(0, step).wait_send()

        for d in (1, 2, 3):
            @pl.when(chip + d < chips)
            def _():
                pair_of(d, step, core).wait_send()
                part_of(d, step).wait_send()
                up(d, step).wait_send()
                if d == 3:
                    relay(step).wait_send()

        for frame in (0, 1):
            @pl.when(head != frame * 2 + step // 2 % 2)
            def _():
                swap(step, frame).wait_send()

    for stage, size in enumerate(stage_sizes):
        for at in range(size):
            weigh(stage, at).wait_send()


def per_device(query, keys, values, out_weight, radius, block_mask):
    width = out_weight.shape[1]
    scale = math.log2(math.e) / math.sqrt(128)
    bf16 = jnp.bfloat16
    dma = pltpu.SemaphoreType.DMA
    mixed = pl.pallas_call(
        functools.partial(attend, scale),
        out_shape=jax.ShapeDtypeStruct((128, width), bf16),
        in_specs=[pl.BlockSpec(memory_space=pl.ANY)] * 6,
        out_specs=pl.BlockSpec(memory_space=pltpu.VMEM),
        scratch_shapes=[
            pltpu.VMEM((512, 384), bf16),
            pltpu.VMEM((512, 384), bf16),
            pltpu.VMEM((512, 384), bf16),
            pltpu.SMEM((3,), jnp.int32),
            pltpu.SMEM((3, 8, 8), jnp.int32),
            pltpu.VMEM((2, 3, 6, 6, 32, 128), bf16),
            pltpu.VMEM((4, 2, STEPS, 128, 128), bf16),
            pltpu.VMEM((4, 2, STEPS, ROWS, 128), bf16),
            pltpu.VMEM((4, STEPS, ROWS, 128), bf16),
            pltpu.VMEM((3, STEPS, ROWS, 128), bf16),
            pltpu.VMEM((3, STEPS, ROWS, 128), bf16),
            pltpu.VMEM((STEPS, 2, 64, 128), bf16),
            pltpu.VMEM((4, 3, 2, 64, 128), bf16),
            pltpu.VMEM((STEPS, 128, 512), jnp.float32),
            pltpu.VMEM((2, 16, 4, 3, 16, 384), bf16),
            pltpu.VMEM((128, width), jnp.float32),
            dma((6,)),
            dma((8,)), dma((8,)),
            dma((3, STEPS)), dma((3, STEPS)),
            dma((4, STEPS)), dma((4, STEPS)),
            dma((4, STEPS)), dma((4, STEPS)),
            dma((3, STEPS)), dma((3, STEPS)),
            dma((STEPS, 2)), dma((4, 3, 2)),
            dma((4, 3)), dma((4, 3)),
        ],
        compiler_params=pltpu.CompilerParams(
            collective_id=0, has_side_effects=True, vmem_limit_bytes=60 * 1024 * 1024
        ),
        cost_estimate=pl.CostEstimate(flops=6_400_000_000, bytes_accessed=2_000_000, transcendentals=6_000_000),
        name="attend",
    )(
        query.reshape(512, 384), keys.reshape(512, 384), values.reshape(512, 384),
        out_weight.reshape(3, 8, 16, width), radius, block_mask,
    )
    return mixed.reshape(1, 1, 128, width)


def solution(mesh):
    in_specs = (
        P("tm", "tile", None, None, None, "head"),
        P("tm", "tile", None, None, None, "head"),
        P("tm", "tile", None, None, None, "head"),
        P("head", None),
        P("head"),
        P("head", None, None),
    )
    out_specs = P("tm", "tile", "head", None)
    return jax.shard_map(per_device, mesh=mesh, in_specs=in_specs, out_specs=out_specs, check_vma=False)
```
